256 devices in a mesh: expert: 16 (over y, x), tensor: 8 (over z), dp: 2 (over core).
Axes of the slice: x: 4, y: 4, z: 8, core: 2. Of those that a mesh axis runs over, the one named last changes fastest.
Arguments:
- moe_input: bfloat16 [2048, 3072], P('expert', ('tensor', 'dp')), may hold values from -6 to 6
- grad_out: bfloat16 [2048, 3072], P('expert', ('tensor', 'dp')), may hold values from -6 to 6
- expert_ids: int32 [2048, 4], P('expert'), may hold values from 0 to 15, all different within a row; in each aligned block of 128 rows (0 to 127, 128 to 255, ...) at most 64 rows name the same one
- route_weight: float32 [2048, 4], P('expert'), may hold values from 0.1 to 1
- gate_pre: bfloat16 [2048, 4, 6144], P('expert', None, ('tensor', 'dp')), may hold values from -8 to 8
- up_weight: bfloat16 [16, 3072, 6144], P('expert', None, ('tensor', 'dp')), may hold values from -0.109375 to 0.109375
- down_weight: bfloat16 [16, 3072, 6144], P('expert', None, ('tensor', 'dp')), may hold values from -0.078125 to 0.078125
Outputs:
- input_grad: bfloat16 [2048, 3072], P('expert', ('tensor', 'dp'))
- gate_grad: bfloat16 [2048, 4, 6144], P('expert', None, ('tensor', 'dp'))
- up_grad: bfloat16 [16, 3072, 6144], P('expert', None, ('tensor', 'dp'))
- down_grad: bfloat16 [16, 3072, 6144], P('expert', None, ('tensor', 'dp'))
The draws below stay inside these ranges and needn't reach their ends.
Inputs may be any that keep to these rules, and one draw needn't show every extreme that they name: `expert_ids`: each row names 4 different experts. Among the 128 rows of one device (aligned blocks of 128 rows) no expert is named by more than 64 rows, and in every draw some expert is named by exactly 64 rows of some device.
All inputs are finite; a program needn't handle non-finite values.
Results may differ from the reference program's by a relative error of at most 0.02.
Values may be sent and summed in bfloat16 or wider, within the bound.
A program may use at most 128 MiB of HBM per device.

```python
import math
import jax
import jax.numpy as jnp
import numpy as np
from jax import lax

D = 3072
FF = 6144
TOP = 4
TOK_DEV = 128
EXPERTS = 16
CAP = 64
TOKENS = 2048
N_EXPERT = 16
N_TENSOR = 8
N_DP = 2


def block_scale(key, dims, split, low, high):
    factor_of = 1.0
    for dim, blocks in split:
        draws = jax.random.uniform(jax.random.fold_in(jax.random.fold_in(key, 6), dim), (blocks,), jnp.float32, low / len(split), high / len(split))
        factor_of = factor_of * jnp.repeat(jnp.exp(draws), dims[dim] // blocks).reshape((-1,) + (1,) * (len(dims) - 1 - dim))
    return factor_of


def routed_block(stream_key, own, number, rows, amount, top, reach, skew):
    ranking = jax.random.permutation(stream_key, amount)
    packed, common = shares(amount, rows * top, reach, skew, True), shares(amount, rows * top, reach, skew, False)
    places = jnp.arange(amount)

    def named(lengths, turn):
        used = int((lengths > 0).sum())
        fixed = max(1, used // 4)
        passed = fixed + (places - fixed + turn * (used - fixed)) % max(1, amount - fixed)
        return jnp.zeros((amount,), jnp.int32).at[ranking[jnp.where(places < fixed, places, passed)]].set(jnp.asarray(lengths, jnp.int32))

    lengths = jnp.where(number % 4 == 0, named(packed, number // 4), named(common, number - number // 4 - 1))
    mixed = jax.random.permutation(jax.random.fold_in(own, 3), amount)
    donor, sink = mixed[0:amount // 2 * 2:2], mixed[1:amount // 2 * 2:2]
    slack = jnp.minimum(lengths[donor] - 1, reach - lengths[sink]) // 2
    slack = jnp.where((donor == ranking[0]) | (sink == ranking[0]) | (lengths[sink] == 0), 0, jnp.maximum(slack, 0))
    passed = jax.random.randint(jax.random.fold_in(own, 4), (amount // 2,), 0, 1 << 20) % (slack + 1)
    lengths = lengths.at[donor].add(-passed).at[sink].add(passed)
    items = jnp.searchsorted(jnp.cumsum(lengths), jnp.arange(rows * top), side="right").astype(jnp.int32)
    listing = items.reshape(top, rows).T
    listing = listing[jax.random.permutation(jax.random.fold_in(own, 1), rows)]
    turn = jax.random.randint(jax.random.fold_in(own, 2), (rows, 1), 0, top)
    return jnp.take_along_axis(listing, (jnp.arange(top)[None, :] + turn) % top, axis=1)


def shares(number_of, total, bound, lean, full):
    portions = [(1 << 20) // math.isqrt(grade ** lean) + 1 for grade in range(1, number_of + 1)]
    largest = bound if full else min(bound, max(-(-total // number_of), total * portions[0] // sum(portions)))
    least = 1 if total - largest >= number_of - 1 else 0
    counts, surplus = [largest] + [least] * (number_of - 1), total - largest - least * (number_of - 1)
    while surplus > 0:
        free = [i for i in range(1, number_of) if counts[i] < largest] or [i for i in range(1, number_of) if counts[i] < bound]
        whole, left = sum([portions[i] for i in free]), surplus
        for i in free:
            addition = min(bound - counts[i], max(1, left * portions[i] // whole), surplus)
            counts[i] = counts[i] + addition
            surplus = surplus - addition
    return np.array(counts)


def noise(rng, dims, scale, limit, split=(), kind=jnp.bfloat16):
    entries = jax.random.normal(rng, dims, jnp.float32) * scale
    if len(split) > 0:
        entries = block_scale(rng, dims, split, -0.22, 0.18) * entries
    return jnp.clip(entries, min=-limit, max=limit).astype(kind)


def setup_inputs(seed: int = 0) -> dict:
    streams_of = jax.random.split(jax.random.key(seed), 8)
    moe_input = noise(streams_of[0], (TOKENS, D), 1.0, 6.0, ((0, 16), (1, 16)))
    grad_out = noise(streams_of[1], (TOKENS, D), 1.0, 6.0, ((0, 16), (1, 16)))
    expert_ids_keys = jax.random.split(jax.random.fold_in(streams_of[2], 1), TOKENS // TOK_DEV)
    expert_ids_turns = jax.random.permutation(jax.random.fold_in(streams_of[2], 3), TOKENS // TOK_DEV)
    expert_ids = jax.vmap(lambda own, number: routed_block(jax.random.fold_in(streams_of[2], 2), own, number, TOK_DEV, EXPERTS, TOP, CAP, 2))(expert_ids_keys, expert_ids_turns).reshape((TOKENS, TOP))
    route_weight = jnp.clip(0.1 + 0.9 * jax.random.uniform(streams_of[3], (TOKENS, TOP), jnp.float32) ** block_scale(streams_of[3], (TOKENS, TOP), ((0, 16),), -0.2, 0.2), 0.1, 1.0)
    gate_pre = noise(streams_of[4], (TOKENS, TOP, FF), 1.5, 8.0, ((0, 16), (2, 16)))
    up_weight = noise(streams_of[5], (EXPERTS, D, FF), D ** -0.5, 0.109375, ((0, 16), (2, 16)))
    down_weight = noise(streams_of[6], (EXPERTS, D, FF), FF ** -0.5, 0.078125, ((0, 16), (2, 16)))
    return dict(moe_input=moe_input, grad_out=grad_out, expert_ids=expert_ids, route_weight=route_weight, gate_pre=gate_pre, up_weight=up_weight, down_weight=down_weight)


def silu_terms(gate_value):
    sigmoid = jax.nn.sigmoid(gate_value)
    return gate_value * sigmoid, sigmoid * (1.0 + gate_value * (1.0 - sigmoid))


def reference(moe_input, grad_out, expert_ids, route_weight, gate_pre, up_weight, down_weight):
    shard_count = N_TENSOR * N_DP
    slot_total = CAP * N_EXPERT
    shard_width = FF // shard_count

    def per_expert(expert):
        is_routed = expert_ids == expert
        token_hit = jnp.any(is_routed, axis=1)
        row_index = jnp.nonzero(token_hit, size=slot_total, fill_value=0)[0].astype(jnp.int32)
        valid = jnp.arange(slot_total) < jnp.sum(token_hit.astype(jnp.int32))
        hit_rows = is_routed[row_index]
        route_pos = jnp.sum(jnp.where(hit_rows, jnp.arange(TOP, dtype=jnp.int32)[None, :], 0), axis=1).astype(jnp.int32)
        weight = jnp.sum(jnp.where(hit_rows, route_weight[row_index], 0.0), axis=1)
        weight = jnp.where(valid, weight, 0.0)
        input_rows = jnp.where(valid[:, None], moe_input[row_index], 0)
        dout = (weight[:, None] * grad_out[row_index].astype(jnp.float32)).astype(jnp.bfloat16)
        gate_value = jnp.where(valid[:, None], gate_pre[row_index, route_pos], 0).astype(jnp.float32)
        w_up = up_weight[expert]
        w_down = down_weight[expert]
        up = jnp.dot(input_rows, w_up, preferred_element_type=jnp.float32)
        act, slope = silu_terms(gate_value)
        hidden = (act * up).astype(jnp.bfloat16)
        dhid = jnp.dot(dout, w_down, preferred_element_type=jnp.float32)
        up_delta = (dhid * act).astype(jnp.bfloat16)
        gate_delta = (dhid * up * slope).astype(jnp.bfloat16)
        delta_split = up_delta.astype(jnp.float32).reshape(slot_total, shard_count, shard_width)
        weight_split = w_up.astype(jnp.float32).reshape(D, shard_count, shard_width)
        partial_value = jnp.einsum("snf,dnf->snd", delta_split, weight_split).astype(jnp.bfloat16)
        partial_sum = jnp.sum(partial_value.astype(jnp.float32), axis=1)
        up_grad = lax.dot_general(input_rows, up_delta, (((0,), (0,)), ((), ())), preferred_element_type=jnp.float32).astype(jnp.bfloat16)
        down_grad = lax.dot_general(dout, hidden, (((0,), (0,)), ((), ())), preferred_element_type=jnp.float32).astype(jnp.bfloat16)
        return partial_sum, gate_delta, row_index, route_pos, up_grad, down_grad

    partials, gate_deltas, row_all, pos_all, up_grad, down_grad = lax.map(per_expert, jnp.arange(EXPERTS, dtype=jnp.int32))
    flat_rows = row_all.reshape(-1).astype(jnp.int32)
    flat_pos = pos_all.reshape(-1).astype(jnp.int32)
    input_total = grad_out.astype(jnp.float32).at[flat_rows].add(partials.reshape(-1, D))
    input_grad = input_total.astype(jnp.bfloat16)
    gate_grad = jnp.zeros((TOKENS, TOP, FF), jnp.bfloat16).at[flat_rows, flat_pos].add(gate_deltas.reshape(-1, FF))
    return input_grad, gate_grad, up_grad, down_grad
```

```python
import functools

import jax
import jax.numpy as jnp
from jax import lax
from jax.experimental import pallas as pl
from jax.experimental.pallas import tpu as pltpu
from jax.sharding import PartitionSpec as P

MESH = pl.DeviceIdType.MESH
F32 = jnp.float32
BF16 = jnp.bfloat16
NE = 16
CAP = 64
TOK = 128
ROWS = NE * CAP
CH = 384
GROUP = 256
GROUPS = ROWS // GROUP
PER = GROUP // CAP
NT = (((1,), (1,)), ((), ()))
TN = (((0,), (0,)), ((), ()))


def xor(a, b):
    total = 0
    for bit in (1, 2, 4, 8):
        total = total + bit * lax.rem(lax.div(a, bit) + lax.div(b, bit), 2)
    return total


def block(k):
    return pl.ds(pl.multiple_of(k * CAP, CAP), CAP)


def group_rows(g):
    return pl.ds(pl.multiple_of(g * GROUP, GROUP), GROUP)


def kernel(
    x_ref, g_ref, ids_ref, w_ref, gate_ref, wu_hbm, wd_hbm,
    ig_ref, gg_ref, ug_hbm, dg_hbm,
    wu, wd, s_tok, s_route, w_slot, swap_out, swap_in, t4, slots, xd,
    gate_out, gate_in, gd_out, gd_in, up_s, hid, upd, ps, qd, zs, zr, xs, tr, tk, fr, grads,
    w_sem, swap_sem, a1_s, a1_r, gate_s, gate_r, xy_s, xy_r, za_s, za_r, zb_s, zb_r,
    own_s, own_r, opp_s, opp_r, rd_s, rd_r, rza_s, rza_r, rzb_s, rzb_r, rx_s, rx_r,
    rg_s, rg_r, fin_s, fin_r, out_sem,
):
    me = lax.axis_index("expert")
    z = lax.axis_index("tensor")
    c = lax.axis_index("dp")
    p = lax.rem(z, 2)
    mz = lax.div(z, 2)
    sib = 1 - c
    right = lax.rem(z + 1, 8)
    left = lax.rem(z + 7, 8)

    def copy(src, dst, send, recv, **ids):
        return pltpu.make_async_remote_copy(
            src_ref=src, dst_ref=dst, send_sem=send, recv_sem=recv, device_id=ids, device_id_type=MESH
        )

    bar = pltpu.get_barrier_semaphore()

    def greet(**ids):
        pl.semaphore_signal(bar, inc=1, device_id=ids, device_id_type=MESH)

    greet(dp=sib)
    for j in range(1, 4):
        greet(tensor=lax.rem(z + 2 * j, 8))
        greet(tensor=lax.rem(z + 2 * j, 8), dp=sib)
    greet(tensor=right)
    greet(tensor=left)

    @pl.loop(1, NE)
    def _(k):
        greet(expert=xor(me, k))

    def weight_copies():
        made = []
        for i, (src, dst) in enumerate(((wu_hbm, wu), (wd_hbm, wd))):
            for q in range(8):
                made.append(
                    pltpu.make_async_copy(
                        src.at[0, pl.ds(q * CH, CH)],
                        dst.at[q % 2, pl.ds((q // 2) * CH, CH)],
                        w_sem.at[i * 8 + q],
                    )
                )
        return made

    for made in weight_copies():
        made.start()

    lane = lax.broadcasted_iota(jnp.int32, (TOK, TOK), 1)
    sub = lax.broadcasted_iota(jnp.int32, (TOK, TOK), 0)
    ids = ids_ref[...].astype(F32)
    wts = w_ref[...]
    ids_pad = jnp.zeros((TOK, TOK), F32)
    w_pad = jnp.zeros((TOK, TOK), F32)
    for j in range(4):
        ids_pad = jnp.where(lane == j, ids[:, j : j + 1], ids_pad)
        w_pad = jnp.where(lane == j, wts[:, j : j + 1], w_pad)
    ids_t = ids_pad.T[0:8]
    w_t = w_pad.T[0:8]
    earlier = (sub < lane).astype(BF16)
    hits = []
    experts = [xor(me, k).astype(F32) for k in range(NE)]
    for k in range(NE):
        hits.append([(ids_t[j : j + 1] == experts[k]).astype(F32) for j in range(4)])
    named = jnp.concatenate([h[0] + h[1] + h[2] + h[3] for h in hits], axis=0)
    rank = jnp.dot(named.astype(BF16), earlier, preferred_element_type=F32)
    place = lax.broadcasted_iota(jnp.int32, (CAP, TOK), 0).astype(F32)
    for k in range(NE):
        here = jnp.where((rank[k : k + 1] == place) & (named[k : k + 1] > 0.5), 1.0, 0.0)
        rows = slice(k * CAP, (k + 1) * CAP)
        s_tok[rows] = here.astype(BF16)
        weight = jnp.zeros((1, TOK), F32)
        for j in range(4):
            s_route[rows, j * TOK : (j + 1) * TOK] = (here * hits[k][j]).astype(BF16)
            weight = weight + hits[k][j] * w_t[j : j + 1]
        col = jnp.sum(here * weight, axis=1, keepdims=True)
        w_slot[rows] = jnp.where(c == 0, jnp.ones((CAP, TOK), F32), jnp.broadcast_to(col, (CAP, TOK)))

    pl.semaphore_wait(bar, 24)

    xv = x_ref[...].astype(F32)
    gv = g_ref[...].astype(F32)
    is0 = c == 0
    own_half = jnp.where(is0, xv, gv)
    swap_out[...] = jnp.where(is0, gv, xv).astype(BF16)
    swap = copy(swap_out, swap_in, swap_sem.at[0], swap_sem.at[1], dp=sib)
    swap.start()

    def gate_copy(k):
        return copy(gate_out.at[block(k)], gate_in.at[block(k)], gate_s.at[k], gate_r.at[k], expert=xor(me, k))

    swap.wait_recv()
    got = swap_in[...].astype(F32)
    t4[mz] = jnp.concatenate(
        [jnp.where(is0, own_half, got), jnp.where(is0, got, own_half)], axis=1
    ).astype(BF16)

    def a1_copy(j):
        return copy(t4.at[mz], t4.at[mz], a1_s.at[j - 1], a1_r.at[j - 1], tensor=lax.rem(z + 2 * j, 8))

    for j in (2, 1, 3):
        a1_copy(j).start()

    @pl.loop(0, GROUPS)
    def _(g):
        value = jnp.dot(s_route[group_rows(g)], gate_ref[...], preferred_element_type=F32)
        gate_out[group_rows(g)] = value.astype(BF16)

        @pl.when(g == 0)
        def _():
            gate_in[0:CAP] = value[0:CAP].astype(BF16)

        for i in range(PER):
            k = g * PER + i

            @pl.when(k > 0)
            def _():
                gate_copy(k).start()

    def a1_arrival(j):
        src = lax.rem(mz + 4 - j, 4)
        return copy(t4.at[src], t4.at[src], a1_s.at[j - 1], a1_r.at[j - 1], tensor=lax.rem(z + 2 * j, 8))

    for j in (1, 3, 2):
        a1_arrival(j).wait_recv()

    def xy_copy(k):
        return copy(slots.at[block(k)], xd.at[c, p, block(k)], xy_s.at[k], xy_r.at[k], expert=xor(me, k))

    @pl.loop(0, GROUPS)
    def _(g):
        rows = group_rows(g)
        for m in range(4):
            value = jnp.dot(s_tok[rows], t4[m], preferred_element_type=F32)
            scale = w_slot[rows]
            value = (value * jnp.concatenate([scale] * (CH // TOK), axis=1)).astype(BF16)
            slots[rows, m * CH : (m + 1) * CH] = value

            @pl.when(g == 0)
            def _():
                xd[c, p, 0:CAP, m * CH : (m + 1) * CH] = value[0:CAP]

        for i in range(PER):
            k = g * PER + i

            @pl.when(k > 0)
            def _():
                xy_copy(k).start()

    def za_copy(k, par):
        at = xd.at[c, par, block(k), pl.ds(0, 768)]
        return copy(at, at, za_s.at[k], za_r.at[k], tensor=right)

    def zb_copy(k, par):
        at = xd.at[c, par, block(k), pl.ds(768, 768)]
        return copy(at, at, zb_s.at[k], zb_r.at[k], tensor=left)

    def own_copy(k, arr):
        at = xd.at[arr, p, block(k)]
        return copy(at, at, own_s.at[k], own_r.at[k], dp=sib)

    def opp_copy(k, arr):
        at = xd.at[arr, 1 - p, block(k)]
        return copy(at, at, opp_s.at[k], opp_r.at[k], dp=sib)

    def rd_copy(g):
        return copy(ps.at[sib, g], qd.at[g], rd_s.at[g], rd_r.at[g], dp=sib)

    def rza_copy(g):
        return copy(zs.at[g, 0], zr.at[g, 0], rza_s.at[g], rza_r.at[g], tensor=right)

    def rzb_copy(g):
        return copy(zs.at[g, 1], zr.at[g, 1], rzb_s.at[g], rzb_r.at[g], tensor=left)

    def rx_copy(k):
        return copy(xs.at[:, block(k)], tr.at[:, block(k)], rx_s.at[k], rx_r.at[k], expert=xor(me, k))

    def rg_copy(k):
        return copy(gd_out.at[block(k)], gd_in.at[block(k)], rg_s.at[k], rg_r.at[k], expert=xor(me, k))

    def compute_up(g):
        rows = group_rows(g)

        @pl.when(g == 0)
        def _():
            for made in weight_copies():
                made.wait()

        up_s[...] = jnp.dot(xd[0, 0, rows], wu[0], preferred_element_type=F32) + jnp.dot(
            xd[0, 1, rows], wu[1], preferred_element_type=F32
        )

    def compute_down(g):
        rows = group_rows(g)
        for i in range(PER):
            k = g * PER + i

            @pl.when(k > 0)
            def _():
                gate_copy(k).wait_recv()

        dhid = jnp.dot(xd[1, 0, rows], wd[0], preferred_element_type=F32) + jnp.dot(
            xd[1, 1, rows], wd[1], preferred_element_type=F32
        )
        up = up_s[...]
        gate = gate_in[rows].astype(F32)
        s = 1.0 / (1.0 + jnp.exp(-gate))
        act = gate * s
        hid[rows] = (act * up).astype(BF16)
        upd[rows] = (dhid * act).astype(BF16)
        delta = (dhid * up * (s * (1.0 + gate * (1.0 - s)))).astype(BF16)
        gd_out[rows] = delta

        @pl.when(g == 0)
        def _():
            gd_in[0:CAP] = delta[0:CAP]

        for i in range(PER):
            k = g * PER + i

            @pl.when(k > 0)
            def _():
                rg_copy(k).start()

    def compute_partial(g):
        value = upd[group_rows(g)]
        for m in range(4):
            for par in range(2):
                ps[m % 2, g, par, m // 2] = lax.dot_general(
                    value, wu[par, m * CH : (m + 1) * CH], NT, preferred_element_type=F32
                ).astype(BF16)
        rd_copy(g).start()

    def return_z(g):
        rd_copy(g).wait_recv()
        for mm in range(2):
            total = ps[c, g, 1 - p, mm].astype(F32) + qd[g, 1 - p, mm].astype(F32)
            zs[g, mm] = total.astype(BF16)
        rza_copy(g).start()
        rzb_copy(g).start()

    def return_xy(g):
        rza_copy(g).wait_recv()
        rzb_copy(g).wait_recv()
        rows = group_rows(g)
        for mm in range(2):
            total = ps[c, g, p, mm].astype(F32) + qd[g, p, mm].astype(F32) + zr[g, mm].astype(F32)
            value = total.astype(BF16)
            xs[mm, rows] = value

            @pl.when(g == 0)
            def _():
                tr[mm, 0:CAP] = value[0:CAP]

        for i in range(PER):
            k = g * PER + i

            @pl.when(k > 0)
            def _():
                rx_copy(k).start()

    def grad(a, par, m):
        left_side = xd[a, par, :, m * CH : (m + 1) * CH]
        right_side = (upd if a == 0 else hid)[...]
        q = 2 * m + par
        rows = slice(q * CH, (q + 1) * CH)
        grads[a, rows] = lax.dot_general(left_side, right_side, TN, preferred_element_type=F32).astype(BF16)
        grad_copy(a, q).start()

    def grad_copy(a, q):
        rows = pl.ds(q * CH, CH)
        return pltpu.make_async_copy(grads.at[a, rows], (ug_hbm, dg_hbm)[a].at[0, rows], out_sem.at[a * 8 + q])

    jobs = [(a, par, m) for a in range(2) for m in range(4) for par in range(2)]
    LAG_Z, LAG_S, LAG_C = 2, 3, 4
    FIRST = PER - 1 + LAG_C

    @pl.loop(0, FIRST + 4 * (GROUPS - 1) + 3)
    def _(step):
        @pl.when(step < NE)
        def _():
            @pl.when(step > 0)
            def _():
                xy_copy(step).wait_recv()

            za_copy(step, p).start()
            zb_copy(step, p).start()
            own_copy(step, c).start()

        @pl.when((step >= LAG_Z) & (step < NE + LAG_Z))
        def _():
            k = step - LAG_Z
            za_copy(k, 1 - p).wait_recv()
            zb_copy(k, 1 - p).wait_recv()
            opp_copy(k, c).start()

        @pl.when((step >= LAG_S) & (step < NE + LAG_S))
        def _():
            k = step - LAG_S
            own_copy(k, sib).wait_recv()
            opp_copy(k, sib).wait_recv()

        @pl.when(step >= FIRST)
        def _():
            turn = step - FIRST
            g = lax.div(turn, 4)
            phase = lax.rem(turn, 4)

            @pl.when(phase == 0)
            def _():
                compute_up(g)

                @pl.when(g > 0)
                def _():
                    return_xy(g - 1)

            @pl.when(phase == 1)
            def _():
                compute_down(g)

            @pl.when(phase == 2)
            def _():
                compute_partial(g)

            @pl.when(phase == 3)
            def _():
                return_z(g)

    last = GROUPS - 1
    for job in jobs[0:3]:
        grad(*job)
    return_z(last)
    for job in jobs[3:7]:
        grad(*job)
    return_xy(last)
    for job in jobs[7:12]:
        grad(*job)

    @pl.loop(1, NE)
    def _(k):
        rx_copy(k).wait_recv()

    def fin_dest(mm):
        return 2 * (c + 2 * mm) + p

    def fin_copy(mm, h):
        return copy(
            tk.at[mm, h], fr.at[mz], fin_s.at[mm * 2 + h], fin_r.at[mz], tensor=fin_dest(mm), dp=jnp.int32(h)
        )

    def fin_local(mm, h):
        return (fin_dest(mm) == z) & (c == h)

    for mm in range(2):
        total = lax.dot_general(s_tok[...], tr[mm], TN, preferred_element_type=F32)
        for h in range(2):
            value = total[:, h * 192 : (h + 1) * 192].astype(BF16)
            tk[mm, h] = value

            @pl.when(fin_local(mm, h))
            def _():
                fr[mz] = value

            @pl.when(jnp.logical_not(fin_local(mm, h)))
            def _():
                fin_copy(mm, h).start()

    for job in jobs[12:16]:
        grad(*job)

    @pl.loop(1, NE)
    def _(k):
        rg_copy(k).wait_recv()

    gg_ref[...] = lax.dot_general(s_route[...], gd_in[...], TN, preferred_element_type=F32).astype(BF16)

    swap.wait_send()
    for j in range(1, 4):
        a1_copy(j).wait_send()

    @pl.loop(0, NE)
    def _(k):
        za_copy(k, p).wait_send()
        zb_copy(k, p).wait_send()
        own_copy(k, c).wait_send()
        opp_copy(k, c).wait_send()

        @pl.when(k > 0)
        def _():
            gate_copy(k).wait_send()
            xy_copy(k).wait_send()
            rx_copy(k).wait_send()
            rg_copy(k).wait_send()

    @pl.loop(0, GROUPS)
    def _(g):
        rd_copy(g).wait_send()
        rza_copy(g).wait_send()
        rzb_copy(g).wait_send()

    for a in range(2):
        for q in range(8):
            grad_copy(a, q).wait()

    for src in range(4):
        @pl.when(jnp.logical_not((mz == src) & (c == lax.rem(mz, 2))))
        def _():
            copy(
                fr.at[src], fr.at[src], fin_s.at[0], fin_r.at[src], tensor=right
            ).wait_recv()

    total = g_ref[...].astype(F32)
    for src in range(4):
        total = total + fr[src].astype(F32)
    ig_ref[...] = total.astype(BF16)

    for mm in range(2):
        for h in range(2):
            @pl.when(jnp.logical_not(fin_local(mm, h)))
            def _():
                fin_copy(mm, h).wait_send()


def local(moe_input, grad_out, expert_ids, route_weight, gate_pre, up_weight, down_weight):
    gates = jnp.swapaxes(gate_pre, 0, 1).reshape(4 * TOK, CH)
    vmem = pl.BlockSpec(memory_space=pltpu.VMEM)
    anywhere = pl.BlockSpec(memory_space=pl.ANY)
    dma = pltpu.SemaphoreType.DMA

    def scratch(*shape, dtype=BF16):
        return pltpu.VMEM(shape, dtype)

    input_grad, gate_rows, up_grad, down_grad = pl.pallas_call(
        kernel,
        out_shape=(
            jax.ShapeDtypeStruct((TOK, 192), BF16),
            jax.ShapeDtypeStruct((4 * TOK, CH), BF16),
            jax.ShapeDtypeStruct(up_weight.shape, BF16),
            jax.ShapeDtypeStruct(down_weight.shape, BF16),
        ),
        in_specs=[vmem] * 5 + [anywhere] * 2,
        out_specs=(vmem, vmem, anywhere, anywhere),
        scratch_shapes=[
            scratch(2, 4 * CH, CH),
            scratch(2, 4 * CH, CH),
            scratch(ROWS, TOK),
            scratch(ROWS, 4 * TOK),
            scratch(ROWS, TOK, dtype=F32),
            scratch(TOK, 192),
            scratch(TOK, 192),
            scratch(4, TOK, CH),
            scratch(ROWS, 4 * CH),
            scratch(2, 2, ROWS, 4 * CH),
            scratch(ROWS, CH),
            scratch(ROWS, CH),
            scratch(ROWS, CH),
            scratch(ROWS, CH),
            scratch(GROUP, CH, dtype=F32),
            scratch(ROWS, CH),
            scratch(ROWS, CH),
            scratch(2, GROUPS, 2, 2, GROUP, CH),
            scratch(GROUPS, 2, 2, GROUP, CH),
            scratch(GROUPS, 2, GROUP, CH),
            scratch(GROUPS, 2, GROUP, CH),
            scratch(2, ROWS, CH),
            scratch(2, ROWS, CH),
            scratch(2, 2, TOK, 192),
            scratch(4, TOK, 192),
            scratch(2, 8 * CH, CH),
            dma((16,)),
            dma((2,)),
            dma((3,)), dma((3,)),
            dma((NE,)), dma((NE,)),
            dma((NE,)), dma((NE,)),
            dma((NE,)), dma((NE,)),
            dma((NE,)), dma((NE,)),
            dma((NE,)), dma((NE,)),
            dma((NE,)), dma((NE,)),
            dma((GROUPS,)), dma((GROUPS,)),
            dma((GROUPS,)), dma((GROUPS,)),
            dma((GROUPS,)), dma((GROUPS,)),
            dma((NE,)), dma((NE,)),
            dma((NE,)), dma((NE,)),
            dma((4,)), dma((4,)),
            dma((16,)),
        ],
        compiler_params=pltpu.CompilerParams(
            collective_id=0, has_side_effects=True, vmem_limit_bytes=60 * 1024 * 1024
        ),
        name="routed_backward",
    )(moe_input, grad_out, expert_ids, route_weight, gates, up_weight, down_weight)
    gate_grad = jnp.swapaxes(gate_rows.reshape(4, TOK, CH), 0, 1)
    return input_grad, gate_grad, up_grad, down_grad


def solution(mesh):
    sharded = P("expert", ("tensor", "dp"))
    cube = P("expert", None, ("tensor", "dp"))
    rows = P("expert", None)
    return jax.shard_map(
        local,
        mesh=mesh,
        in_specs=(sharded, sharded, rows, rows, cube, cube, cube),
        out_specs=(sharded, cube, cube, cube),
        check_vma=False,
    )
```

```python
import functools

import jax
import jax.numpy as jnp
from jax import lax
from jax.experimental import pallas as pl
from jax.experimental.pallas import tpu as pltpu
from jax.sharding import PartitionSpec as P

MESH = pl.DeviceIdType.MESH
F32 = jnp.float32
BF16 = jnp.bfloat16
NE = 16
CAP = 64
TOK = 128
ROWS = NE * CAP
CH = 384
GROUP = 256
WINDOW = 8
GROUPS = ROWS // GROUP
PER = GROUP // CAP
NT = (((1,), (1,)), ((), ()))
TN = (((0,), (0,)), ((), ()))


def partner(me, k):
    k0, k1, k2, k3 = (lax.rem(lax.div(k, bit), 2) for bit in (1, 2, 4, 8))
    flips = (k0 + k1 + k2, k1 + k3, k0 + k1, k1)
    total = 0
    for i, flip in enumerate(flips):
        total = total + 2**i * lax.rem(lax.div(me, 2**i) + flip, 2)
    return total


def block(k):
    return pl.ds(pl.multiple_of(k * CAP, CAP), CAP)


def group_rows(g):
    return pl.ds(pl.multiple_of(g * GROUP, GROUP), GROUP)


def kernel(
    x_hbm, g_hbm, ids_hbm, w_hbm, gate_hbm, wu_hbm, wd_hbm,
    ig_ref, gg_ref, ug_hbm, dg_hbm,
    inp, ids_ref, w_ref, gate_ref,
    wu, wd, s_tok, s_route, w_slot, t4, slots, xd,
    gate_out, gate_in, gd_out, gd_in, up_s, hid, upd, ps, qd, zs, zr, xs, tr, tk, fr, grads,
    in_sem, w_sem, swap_sem, a1_s, a1_r, gate_s, gate_r, xy_s, xy_r, za_s, za_r, zb_s, zb_r,
    own_s, own_r, opp_s, opp_r, rd_s, rd_r, rza_s, rza_r, rzb_s, rzb_r, rx_s, rx_r,
    rg_s, rg_r, fin_s, fin_r, out_sem,
):
    me = lax.axis_index("expert")
    z = lax.axis_index("tensor")
    c = lax.axis_index("dp")
    p = lax.rem(z, 2)
    mz = lax.div(z, 2)
    sib = 1 - c
    right = lax.rem(z + 1, 8)
    left = lax.rem(z + 7, 8)

    def copy(src, dst, send, recv, **ids):
        return pltpu.make_async_remote_copy(
            src_ref=src, dst_ref=dst, send_sem=send, recv_sem=recv, device_id=ids, device_id_type=MESH
        )

    loads = [
        pltpu.make_async_copy(src, dst, in_sem.at[i])
        for i, (src, dst) in enumerate(
            ((ids_hbm, ids_ref), (w_hbm, w_ref), (x_hbm, inp.at[0]), (g_hbm, inp.at[1]), (gate_hbm, gate_ref))
        )
    ]
    for load in loads:
        load.start()

    bar = pltpu.get_barrier_semaphore()

    def greet(**ids):
        pl.semaphore_signal(bar, inc=1, device_id=ids, device_id_type=MESH)

    greet(dp=sib)
    for j in range(1, 4):
        greet(tensor=lax.rem(z + 2 * j, 8))
        greet(tensor=lax.rem(z + 2 * j, 8), dp=sib)
    greet(tensor=right)
    greet(tensor=left)

    @pl.loop(1, NE)
    def _(k):
        greet(expert=partner(me, k))

    def weight_copies():
        made = []
        for i, (src, dst) in enumerate(((wu_hbm, wu), (wd_hbm, wd))):
            for q in range(8):
                made.append(
                    pltpu.make_async_copy(
                        src.at[0, pl.ds(q * CH, CH)],
                        dst.at[q % 2, pl.ds((q // 2) * CH, CH)],
                        w_sem.at[i * 8 + q],
                    )
                )
        return made

    for made in weight_copies():
        made.start()

    loads[0].wait()
    loads[1].wait()
    lane = lax.broadcasted_iota(jnp.int32, (TOK, TOK), 1)
    sub = lax.broadcasted_iota(jnp.int32, (TOK, TOK), 0)
    earlier = (sub < lane).astype(BF16)
    lane4 = lax.broadcasted_iota(jnp.int32, (TOK, 4 * TOK), 1)
    sub4 = 4 * lax.broadcasted_iota(jnp.int32, (TOK, 4 * TOK), 0)
    spread = ((lane4 >= sub4) & (lane4 < sub4 + 4)).astype(BF16)
    ids = ids_ref[...].astype(F32)
    wts = w_ref[...]
    experts = [partner(me, jnp.int32(k)).astype(F32) for k in range(NE)]
    hits = [[(ids[j : j + 1] == experts[k]).astype(F32) for j in range(4)] for k in range(NE)]
    named = jnp.concatenate([h[0] + h[1] + h[2] + h[3] for h in hits], axis=0)
    rank = jnp.dot(named.astype(BF16), earlier, preferred_element_type=F32)
    rank4 = jnp.dot(rank.astype(BF16), spread, preferred_element_type=F32)
    ids_wide = jnp.dot(
        jnp.concatenate([ids, ids], axis=0).astype(BF16), spread, preferred_element_type=F32
    )
    route = lax.rem(lax.broadcasted_iota(jnp.int32, (1, 4 * TOK), 1), 4)
    ids4 = jnp.zeros((1, 4 * TOK), F32)
    for j in range(4):
        ids4 = jnp.where(route == j, ids_wide[j : j + 1], ids4)
    place = lax.broadcasted_iota(jnp.int32, (CAP, TOK), 0).astype(F32)
    place4 = lax.broadcasted_iota(jnp.int32, (CAP, 4 * TOK), 0).astype(F32)
    for k in range(NE):
        here = jnp.where((rank[k : k + 1] == place) & (named[k : k + 1] > 0.5), 1.0, 0.0)
        rows = slice(k * CAP, (k + 1) * CAP)
        s_tok[rows] = here.astype(BF16)
        weight = jnp.zeros((1, TOK), F32)
        for j in range(4):
            weight = weight + hits[k][j] * wts[j : j + 1]
        col = jnp.sum(here * weight, axis=1, keepdims=True)
        w_slot[rows] = jnp.where(c == 0, jnp.ones((CAP, TOK), F32), jnp.broadcast_to(col, (CAP, TOK)))
        here4 = jnp.where((rank4[k : k + 1] == place4) & (ids4 == experts[k]), 1.0, 0.0)
        s_route[rows] = here4.astype(BF16)

    loads[2].wait()
    loads[3].wait()

    def half(i):
        return pl.ds(pl.multiple_of(192 * i, 192), 192)

    t4[mz, half(c)] = inp[c]
    pl.semaphore_wait(bar, 24)

    swap = copy(inp.at[sib], t4.at[mz, half(c)], swap_sem.at[0], swap_sem.at[1], dp=sib)
    swap.start()
    copy(inp.at[sib], t4.at[mz, half(sib)], swap_sem.at[0], swap_sem.at[1], dp=sib).wait_recv()

    def a1_copy(j):
        return copy(t4.at[mz], t4.at[mz], a1_s.at[j - 1], a1_r.at[j - 1], tensor=lax.rem(z + 2 * j, 8))

    for j in (2, 1, 3):
        a1_copy(j).start()

    def a1_arrival(j):
        src = lax.rem(mz + 4 - j, 4)
        return copy(t4.at[src], t4.at[src], a1_s.at[j - 1], a1_r.at[j - 1], tensor=lax.rem(z + 2 * j, 8))

    def xy_copy(k, m):
        at = 4 * k + m
        return copy(
            slots.at[m, block(k)], xd.at[c, p, m, block(k)], xy_s.at[at], xy_r.at[at], expert=partner(me, k)
        )

    def fill(g, m):
        rows = group_rows(g)
        value = lax.dot_general(s_tok[rows], t4[m], NT, preferred_element_type=F32)
        scale = w_slot[rows]
        value = (value * jnp.concatenate([scale] * (CH // TOK), axis=1)).astype(BF16)
        slots[m, rows] = value

        @pl.when(g == 0)
        def _():
            xd[c, p, m, 0:CAP] = value[0:CAP]

    def gate_copy(k):
        return copy(gate_out.at[block(k)], gate_in.at[block(k)], gate_s.at[k], gate_r.at[k], expert=partner(me, k))

    @pl.loop(0, GROUPS)
    def _(g):
        fill(g, mz)
        for i in range(PER):
            k = g * PER + i

            @pl.when(k > 0)
            def _():
                xy_copy(k, mz).start()

    loads[4].wait()
    gate_rows = gate_ref[...].reshape(4 * TOK, CH)
    for g in range(GROUPS):
        value = jnp.dot(s_route[g * GROUP : (g + 1) * GROUP], gate_rows, preferred_element_type=F32).astype(BF16)
        gate_out[g * GROUP : (g + 1) * GROUP] = value
        if g == 0:
            gate_in[0:CAP] = value[0:CAP]
        for i in range(PER):
            k = g * PER + i
            if k > 0:
                gate_copy(jnp.int32(k)).start()

    for j in (1, 3, 2):
        a1_arrival(j).wait_recv()

    def others():
        return [lax.rem(mz + j, 4) for j in (1, 2, 3)]

    def send(k):
        for m in others():
            xy_copy(k, m).start()

    @pl.loop(0, GROUPS)
    def _(g):
        for m in others():
            fill(g, m)
        for i in range(PER):
            k = g * PER + i

            @pl.when((k > 0) & (k < WINDOW))
            def _():
                send(k)

    def za_copy(k, par):
        at = xd.at[c, par, pl.ds(0, 2), block(k)]
        return copy(at, at, za_s.at[k], za_r.at[k], tensor=right)

    def zb_copy(k, par):
        at = xd.at[c, par, pl.ds(2, 2), block(k)]
        return copy(at, at, zb_s.at[k], zb_r.at[k], tensor=left)

    def own_copy(k, arr):
        at = xd.at[arr, p, :, block(k)]
        return copy(at, at, own_s.at[k], own_r.at[k], dp=sib)

    def opp_copy(k, arr):
        at = xd.at[arr, 1 - p, :, block(k)]
        return copy(at, at, opp_s.at[k], opp_r.at[k], dp=sib)

    def rd_copy(g):
        return copy(ps.at[sib, g], qd.at[g], rd_s.at[g], rd_r.at[g], dp=sib)

    def rza_copy(g):
        return copy(zs.at[g, 0], zr.at[g, 0], rza_s.at[g], rza_r.at[g], tensor=right)

    def rzb_copy(g):
        return copy(zs.at[g, 1], zr.at[g, 1], rzb_s.at[g], rzb_r.at[g], tensor=left)

    def rx_copy(k):
        return copy(xs.at[:, block(k)], tr.at[:, block(k)], rx_s.at[k], rx_r.at[k], expert=partner(me, k))

    def rg_copy(k):
        return copy(gd_out.at[block(k)], gd_in.at[block(k)], rg_s.at[k], rg_r.at[k], expert=partner(me, k))

    def product(a, weights, rows):
        total = None
        for par in range(2):
            wide = jnp.concatenate([xd[a, par, m, rows] for m in range(4)], axis=1)
            term = jnp.dot(wide, weights[par], preferred_element_type=F32)
            total = term if total is None else total + term
        return total

    def compute_up(g):
        @pl.when(g == 0)
        def _():
            for made in weight_copies():
                made.wait()

        up_s[...] = product(0, wu, group_rows(g))

    def compute_down(g):
        rows = group_rows(g)
        for i in range(PER):
            k = g * PER + i

            @pl.when(k > 0)
            def _():
                gate_copy(k).wait_recv()

        dhid = product(1, wd, rows)
        up = up_s[...]
        gate = gate_in[rows].astype(F32)
        s = 1.0 / (1.0 + jnp.exp(-gate))
        act = gate * s
        hid[rows] = (act * up).astype(BF16)
        upd[rows] = (dhid * act).astype(BF16)
        delta = (dhid * up * (s * (1.0 + gate * (1.0 - s)))).astype(BF16)
        gd_out[rows] = delta

        @pl.when(g == 0)
        def _():
            gd_in[0:CAP] = delta[0:CAP]

        for i in range(PER):
            k = g * PER + i

            @pl.when(k > 0)
            def _():
                rg_copy(k).start()

    def compute_partial(g):
        value = upd[group_rows(g)]
        for m in range(4):
            for par in range(2):
                ps[m % 2, g, par, m // 2] = lax.dot_general(
                    value, wu[par, m * CH : (m + 1) * CH], NT, preferred_element_type=F32
                ).astype(BF16)
        rd_copy(g).start()

    def return_z(g):
        rd_copy(g).wait_recv()
        for mm in range(2):
            total = ps[c, g, 1 - p, mm].astype(F32) + qd[g, 1 - p, mm].astype(F32)
            zs[g, mm] = total.astype(BF16)
        rza_copy(g).start()
        rzb_copy(g).start()

    def return_xy(g):
        rza_copy(g).wait_recv()
        rzb_copy(g).wait_recv()
        rows = group_rows(g)
        for mm in range(2):
            total = ps[c, g, p, mm].astype(F32) + qd[g, p, mm].astype(F32) + zr[g, mm].astype(F32)
            value = total.astype(BF16)
            xs[mm, rows] = value

            @pl.when(g == 0)
            def _():
                tr[mm, 0:CAP] = value[0:CAP]

        for i in range(PER):
            k = g * PER + i

            @pl.when(k > 0)
            def _():
                rx_copy(k).start()

    def grad(a, par, m):
        right_side = (upd if a == 0 else hid)[...]
        q = 2 * m + par
        rows = slice(q * CH, (q + 1) * CH)
        grads[a, rows] = lax.dot_general(xd[a, par, m], right_side, TN, preferred_element_type=F32).astype(BF16)
        grad_copy(a, q).start()

    def grad_copy(a, q):
        rows = pl.ds(q * CH, CH)
        return pltpu.make_async_copy(grads.at[a, rows], (ug_hbm, dg_hbm)[a].at[0, rows], out_sem.at[a * 8 + q])

    jobs = [(a, par, m) for a in range(2) for m in range(4) for par in range(2)]
    LAG_Z, LAG_S, LAG_C = 2, 3, 4
    FIRST = PER - 1 + LAG_C

    @pl.loop(0, FIRST + 4 * (GROUPS - 1) + 3)
    def _(step):
        @pl.when(step < NE)
        def _():
            @pl.when(step > 0)
            def _():
                for m in range(4):
                    xy_copy(step, m).wait_recv()

            za_copy(step, p).start()
            zb_copy(step, p).start()
            own_copy(step, c).start()

            @pl.when(step + WINDOW < NE)
            def _():
                send(step + WINDOW)

        @pl.when((step >= LAG_Z) & (step < NE + LAG_Z))
        def _():
            k = step - LAG_Z
            za_copy(k, 1 - p).wait_recv()
            zb_copy(k, 1 - p).wait_recv()
            opp_copy(k, c).start()

        @pl.when((step >= LAG_S) & (step < NE + LAG_S))
        def _():
            k = step - LAG_S
            own_copy(k, sib).wait_recv()
            opp_copy(k, sib).wait_recv()

        @pl.when(step >= FIRST)
        def _():
            turn = step - FIRST
            g = lax.div(turn, 4)
            phase = lax.rem(turn, 4)

            @pl.when(phase == 0)
            def _():
                compute_up(g)

                @pl.when(g > 0)
                def _():
                    return_z(g - 1)

            @pl.when(phase == 1)
            def _():
                compute_down(g)

            @pl.when(phase == 2)
            def _():
                compute_partial(g)

                @pl.when(g > 0)
                def _():
                    return_xy(g - 1)

    last = GROUPS - 1
    for job in jobs[0:3]:
        grad(*job)
    return_z(last)
    for job in jobs[3:8]:
        grad(*job)
    return_xy(last)
    for job in jobs[8:14]:
        grad(*job)

    @pl.loop(1, NE)
    def _(k):
        rx_copy(k).wait_recv()

    def fin_dest(mm):
        return 2 * (c + 2 * mm) + p

    def fin_copy(mm, h):
        return copy(
            tk.at[mm, h], fr.at[mz], fin_s.at[mm * 2 + h], fin_r.at[mz], tensor=fin_dest(mm), dp=jnp.int32(h)
        )

    def fin_local(mm, h):
        return (fin_dest(mm) == z) & (c == h)

    for mm in range(2):
        total = lax.dot_general(s_tok[...], tr[mm], TN, preferred_element_type=F32).T
        for h in range(2):
            value = total[h * 192 : (h + 1) * 192].astype(BF16)
            tk[mm, h] = value

            @pl.when(fin_local(mm, h))
            def _():
                fr[mz] = value

            @pl.when(jnp.logical_not(fin_local(mm, h)))
            def _():
                fin_copy(mm, h).start()

    for job in jobs[14:16]:
        grad(*job)

    @pl.loop(1, NE)
    def _(k):
        rg_copy(k).wait_recv()

    gg_ref[...] = (
        lax.dot_general(s_route[...], gd_in[...], TN, preferred_element_type=F32).astype(BF16).reshape(TOK, 4, CH)
    )

    swap.wait_send()
    for j in range(1, 4):
        a1_copy(j).wait_send()

    @pl.loop(0, NE)
    def _(k):
        za_copy(k, p).wait_send()
        zb_copy(k, p).wait_send()
        own_copy(k, c).wait_send()
        opp_copy(k, c).wait_send()

        @pl.when(k > 0)
        def _():
            gate_copy(k).wait_send()
            for m in range(4):
                xy_copy(k, m).wait_send()
            rx_copy(k).wait_send()
            rg_copy(k).wait_send()

    @pl.loop(0, GROUPS)
    def _(g):
        rd_copy(g).wait_send()
        rza_copy(g).wait_send()
        rzb_copy(g).wait_send()

    for a in range(2):
        for q in range(8):
            grad_copy(a, q).wait()

    for src in range(4):
        @pl.when(jnp.logical_not((mz == src) & (c == lax.rem(mz, 2))))
        def _():
            copy(
                fr.at[src], fr.at[src], fin_s.at[0], fin_r.at[src], tensor=right
            ).wait_recv()

    total = inp[1].astype(F32)
    for src in range(4):
        total = total + fr[src].astype(F32)
    ig_ref[...] = total.astype(BF16)

    for mm in range(2):
        for h in range(2):
            @pl.when(jnp.logical_not(fin_local(mm, h)))
            def _():
                fin_copy(mm, h).wait_send()


def finish(ig_in, gg_in, ug_in, dg_in, ig, gg, ug, dg, ig_v, gg_v, ug_v, dg_v, sem_in, sem_out):
    inward, outward = [], []
    for src, mid, dst, parts in (
        (ug_in, ug_v, ug, 4), (dg_in, dg_v, dg, 4), (gg_in, gg_v, gg, 1), (ig_in, ig_v, ig, 1)
    ):
        size = src.shape[1] // parts
        for part in range(parts):
            at = (0, pl.ds(part * size, size)) if parts > 1 else slice(None)
            n = len(inward)
            inward.append(pltpu.make_async_copy(src.at[at], mid.at[at], sem_in.at[n]))
            outward.append(pltpu.make_async_copy(mid.at[at], dst.at[at], sem_out.at[n]))
    for made in inward:
        made.start()
    for arrived, made in zip(inward, outward):
        arrived.wait()
        made.start()
    for made in outward:
        made.wait()


def local(moe_input, grad_out, expert_ids, route_weight, gate_pre, up_weight, down_weight):
    vmem = pl.BlockSpec(memory_space=pltpu.VMEM)
    anywhere = pl.BlockSpec(memory_space=pl.ANY)
    dma = pltpu.SemaphoreType.DMA

    def scratch(*shape, dtype=BF16):
        return pltpu.VMEM(shape, dtype)

    results = pl.pallas_call(
        kernel,
        out_shape=(
            jax.ShapeDtypeStruct((192, TOK), BF16),
            jax.ShapeDtypeStruct((TOK, 4, CH), BF16),
            jax.ShapeDtypeStruct(up_weight.shape, BF16),
            jax.ShapeDtypeStruct(down_weight.shape, BF16),
        ),
        in_specs=[anywhere] * 7,
        out_specs=(vmem, vmem, anywhere, anywhere),
        scratch_shapes=[
            scratch(2, 192, TOK),
            scratch(4, TOK, dtype=jnp.int32),
            scratch(4, TOK, dtype=F32),
            scratch(TOK, 4, CH),
            scratch(2, 4 * CH, CH),
            scratch(2, 4 * CH, CH),
            scratch(ROWS, TOK),
            scratch(ROWS, 4 * TOK),
            scratch(ROWS, TOK, dtype=F32),
            scratch(4, CH, TOK),
            scratch(4, ROWS, CH),
            scratch(2, 2, 4, ROWS, CH),
            scratch(ROWS, CH),
            scratch(ROWS, CH),
            scratch(ROWS, CH),
            scratch(ROWS, CH),
            scratch(GROUP, CH, dtype=F32),
            scratch(ROWS, CH),
            scratch(ROWS, CH),
            scratch(2, GROUPS, 2, 2, GROUP, CH),
            scratch(GROUPS, 2, 2, GROUP, CH),
            scratch(GROUPS, 2, GROUP, CH),
            scratch(GROUPS, 2, GROUP, CH),
            scratch(2, ROWS, CH),
            scratch(2, ROWS, CH),
            scratch(2, 2, 192, TOK),
            scratch(4, 192, TOK),
            scratch(2, 8 * CH, CH),
            dma((5,)),
            dma((16,)),
            dma((2,)),
            dma((3,)), dma((3,)),
            dma((NE,)), dma((NE,)),
            dma((4 * NE,)), dma((4 * NE,)),
            dma((NE,)), dma((NE,)),
            dma((NE,)), dma((NE,)),
            dma((NE,)), dma((NE,)),
            dma((NE,)), dma((NE,)),
            dma((GROUPS,)), dma((GROUPS,)),
            dma((GROUPS,)), dma((GROUPS,)),
            dma((GROUPS,)), dma((GROUPS,)),
            dma((NE,)), dma((NE,)),
            dma((NE,)), dma((NE,)),
            dma((4,)), dma((4,)),
            dma((16,)),
        ],
        compiler_params=pltpu.CompilerParams(
            collective_id=0, has_side_effects=True, vmem_limit_bytes=60 * 1024 * 1024
        ),
        name="routed_backward",
    )(moe_input.T, grad_out.T, expert_ids.T, route_weight.T, gate_pre, up_weight, down_weight)
    input_grad, gate_grad, up_grad, down_grad = pl.pallas_call(
        finish,
        out_shape=tuple(jax.ShapeDtypeStruct(r.shape, r.dtype) for r in results),
        in_specs=[anywhere] * 4,
        out_specs=(anywhere,) * 4,
        scratch_shapes=[scratch(*r.shape) for r in results] + [dma((10,)), dma((10,))],
        compiler_params=pltpu.CompilerParams(vmem_limit_bytes=60 * 1024 * 1024),
        name="results",
    )(*results)
    return input_grad.T, gate_grad, up_grad, down_grad


def solution(mesh):
    sharded = P("expert", ("tensor", "dp"))
    cube = P("expert", None, ("tensor", "dp"))
    rows = P("expert", None)
    return jax.shard_map(
        local,
        mesh=mesh,
        in_specs=(sharded, sharded, rows, rows, cube, cube, cube),
        out_specs=(sharded, cube, cube, cube),
        check_vma=False,
    )
```

```python
import functools

import jax
import jax.numpy as jnp
from jax import lax
from jax.experimental import pallas as pl
from jax.experimental.pallas import tpu as pltpu
from jax.sharding import PartitionSpec as P

MESH = pl.DeviceIdType.MESH
F32 = jnp.float32
BF16 = jnp.bfloat16
NE = 16
CAP = 64
TOK = 128
ROWS = NE * CAP
CH = 384
GROUP = 128
FILL = 256
WINDOW = 8
GROUPS = ROWS // GROUP
PER = GROUP // CAP
NT = (((1,), (1,)), ((), ()))
TN = (((0,), (0,)), ((), ()))


def partner(me, k):
    k0, k1, k2, k3 = (lax.rem(lax.div(k, bit), 2) for bit in (1, 2, 4, 8))
    flips = (k0 + k1 + k2, k1 + k3, k0 + k1, k1)
    total = 0
    for i, flip in enumerate(flips):
        total = total + 2**i * lax.rem(lax.div(me, 2**i) + flip, 2)
    return total


def block(k):
    return pl.ds(pl.multiple_of(k * CAP, CAP), CAP)


def group_rows(g):
    return pl.ds(pl.multiple_of(g * GROUP, GROUP), GROUP)


def kernel(
    x_hbm, g_hbm, ids_hbm, w_hbm, gate_hbm, wu_hbm, wd_hbm,
    ig_ref, gg_ref, ug_hbm, dg_hbm,
    inp, ids_ref, w_ref, gate_ref,
    wu, wd, s_tok, s_route, w_slot, t4, t4_t, slots, xd,
    gate_out, gate_in, gd_out, gd_in, up_s, hid, upd, ps, qd, zs, zr, xs, tr, tk, fr, grads,
    in_sem, w_sem, a1_s, a1_r, gate_s, gate_r, xy_s, xy_r, za_s, za_r, zb_s, zb_r,
    own_s, own_r, opp_s, opp_r, rd_s, rd_r, rza_s, rza_r, rzb_s, rzb_r, rx_s, rx_r,
    rg_s, rg_r, fin_s, fin_r, out_sem,
):
    me = lax.axis_index("expert")
    z = lax.axis_index("tensor")
    c = lax.axis_index("dp")
    p = lax.rem(z, 2)
    mz = lax.div(z, 2)
    sib = 1 - c
    right = lax.rem(z + 1, 8)
    left = lax.rem(z + 7, 8)

    def copy(src, dst, send, recv, **ids):
        return pltpu.make_async_remote_copy(
            src_ref=src, dst_ref=dst, send_sem=send, recv_sem=recv, device_id=ids, device_id_type=MESH
        )

    loads = [
        pltpu.make_async_copy(src, dst, in_sem.at[i])
        for i, (src, dst) in enumerate(
            ((ids_hbm, ids_ref), (w_hbm, w_ref), (x_hbm, inp.at[0]), (g_hbm, inp.at[1]), (gate_hbm, gate_ref))
        )
    ]
    for load in loads:
        load.start()

    bar = pltpu.get_barrier_semaphore()

    def greet(**ids):
        pl.semaphore_signal(bar, inc=1, device_id=ids, device_id_type=MESH)

    greet(dp=sib)
    for j in range(1, 4):
        greet(tensor=lax.rem(z + 2 * j, 8))
        greet(tensor=lax.rem(z + 2 * j, 8), dp=sib)
    greet(tensor=right)
    greet(tensor=left)

    @pl.loop(1, NE)
    def _(k):
        greet(expert=partner(me, k))

    def weight_copies():
        made = []
        for i, (src, dst) in enumerate(((wu_hbm, wu), (wd_hbm, wd))):
            for q in range(8):
                made.append(
                    pltpu.make_async_copy(
                        src.at[0, pl.ds(q * CH, CH)],
                        dst.at[q % 2, pl.ds((q // 2) * CH, CH)],
                        w_sem.at[i * 8 + q],
                    )
                )
        return made

    for made in weight_copies():
        made.start()

    loads[0].wait()
    loads[1].wait()
    lane = lax.broadcasted_iota(jnp.int32, (TOK, TOK), 1)
    sub = lax.broadcasted_iota(jnp.int32, (TOK, TOK), 0)
    earlier = (sub < lane).astype(BF16)
    lane4 = lax.broadcasted_iota(jnp.int32, (TOK, 4 * TOK), 1)
    sub4 = 4 * lax.broadcasted_iota(jnp.int32, (TOK, 4 * TOK), 0)
    spread = ((lane4 >= sub4) & (lane4 < sub4 + 4)).astype(BF16)
    ids = ids_ref[...].astype(F32)
    wts = w_ref[...]
    experts = [partner(me, jnp.int32(k)).astype(F32) for k in range(NE)]
    hits = [[(ids[j : j + 1] == experts[k]).astype(F32) for j in range(4)] for k in range(NE)]
    named = jnp.concatenate([h[0] + h[1] + h[2] + h[3] for h in hits], axis=0)
    rank = jnp.dot(named.astype(BF16), earlier, preferred_element_type=F32)
    rank4 = jnp.dot(rank.astype(BF16), spread, preferred_element_type=F32)
    ids_wide = jnp.dot(
        jnp.concatenate([ids, ids], axis=0).astype(BF16), spread, preferred_element_type=F32
    )
    route = lax.rem(lax.broadcasted_iota(jnp.int32, (1, 4 * TOK), 1), 4)
    ids4 = jnp.zeros((1, 4 * TOK), F32)
    for j in range(4):
        ids4 = jnp.where(route == j, ids_wide[j : j + 1], ids4)
    place = lax.broadcasted_iota(jnp.int32, (CAP, TOK), 0).astype(F32)
    place4 = lax.broadcasted_iota(jnp.int32, (CAP, 4 * TOK), 0).astype(F32)
    for k in range(NE):
        here = jnp.where((rank[k : k + 1] == place) & (named[k : k + 1] > 0.5), 1.0, 0.0)
        rows = slice(k * CAP, (k + 1) * CAP)
        s_tok[rows] = here.astype(BF16)
        weight = jnp.zeros((1, TOK), F32)
        for j in range(4):
            weight = weight + hits[k][j] * wts[j : j + 1]
        col = jnp.sum(here * weight, axis=1, keepdims=True)
        w_slot[rows] = jnp.where(c == 0, jnp.ones((CAP, TOK), F32), jnp.broadcast_to(col, (CAP, TOK)))
        here4 = jnp.where((rank4[k : k + 1] == place4) & (ids4 == experts[k]), 1.0, 0.0)
        s_route[rows] = here4.astype(BF16)

    loads[2].wait()
    loads[3].wait()

    def half(i):
        return pl.ds(pl.multiple_of(192 * i, 192), 192)

    t4[mz, half(c)] = inp[c]
    pl.semaphore_wait(bar, 24)

    def token_copy(j, h):
        return copy(
            inp.at[h], t4.at[mz, half(c)], a1_s.at[2 * j + h], a1_r.at[2 * j + c], tensor=lax.rem(z + 2 * j, 8), dp=h
        )

    def token_arrival(j, h):
        src = lax.rem(mz + 4 - j, 4)
        return copy(
            inp.at[h], t4.at[src, half(h)], a1_s.at[2 * j + h], a1_r.at[2 * j + h], tensor=right, dp=sib
        )

    token_copy(0, sib).start()
    for j in (2, 1, 3):
        token_copy(j, c).start()
        token_copy(j, sib).start()
    token_arrival(0, sib).wait_recv()

    peer = lax.rem(me + 1, NE)

    def xy_copy(k, m, to=peer):
        at = 4 * k + m
        return copy(slots.at[m, block(k)], xd.at[c, p, m, block(k)], xy_s.at[at], xy_r.at[at], expert=to)

    def fill(g, m):
        rows = pl.ds(pl.multiple_of(g * FILL, FILL), FILL)
        value = jnp.dot(s_tok[rows], t4_t[m], preferred_element_type=F32)
        scale = w_slot[rows]
        value = (value * jnp.concatenate([scale] * (CH // TOK), axis=1)).astype(BF16)
        slots[m, rows] = value

        @pl.when(g == 0)
        def _():
            xd[c, p, m, 0:CAP] = value[0:CAP]

    def gate_copy(k, to=peer):
        return copy(gate_out.at[block(k)], gate_in.at[block(k)], gate_s.at[k], gate_r.at[k], expert=to)

    t4_t[mz] = t4[mz].T

    @pl.loop(0, ROWS // FILL)
    def _(g):
        fill(g, mz)
        for i in range(FILL // CAP):
            k = g * (FILL // CAP) + i

            @pl.when(k > 0)
            def _():
                xy_copy(k, mz, partner(me, k)).start()

    loads[4].wait()
    gate_rows = gate_ref[...].reshape(4 * TOK, CH)
    for g in range(4):
        value = jnp.dot(s_route[g * 256 : (g + 1) * 256], gate_rows, preferred_element_type=F32).astype(BF16)
        gate_out[g * 256 : (g + 1) * 256] = value
        if g == 0:
            gate_in[0:CAP] = value[0:CAP]
        if g == 1:
            for k in range(1, 5):
                gate_copy(jnp.int32(k), partner(me, jnp.int32(k))).start()

    for j in (1, 3, 2):
        for h in range(2):
            token_arrival(j, h).wait_recv()
    for j in (1, 3, 2):
        src = lax.rem(mz + 4 - j, 4)
        t4_t[src] = t4[src].T

    def others():
        return [lax.rem(mz + j, 4) for j in (1, 2, 3)]

    def send(k):
        to = partner(me, k)
        for m in others():
            xy_copy(k, m, to).start()

        @pl.when(k > 4)
        def _():
            gate_copy(k, to).start()

    @pl.loop(0, ROWS // FILL)
    def _(g):
        for m in others():
            fill(g, m)
        for i in range(FILL // CAP):
            k = g * (FILL // CAP) + i

            @pl.when((k > 0) & (k < WINDOW))
            def _():
                send(k)

    def za_copy(k, par):
        at = xd.at[c, par, pl.ds(0, 2), block(k)]
        return copy(at, at, za_s.at[k], za_r.at[k], tensor=right)

    def zb_copy(k, par):
        at = xd.at[c, par, pl.ds(2, 2), block(k)]
        return copy(at, at, zb_s.at[k], zb_r.at[k], tensor=left)

    def own_copy(k, arr):
        at = xd.at[arr, p, :, block(k)]
        return copy(at, at, own_s.at[k], own_r.at[k], dp=sib)

    def opp_copy(k, arr):
        at = xd.at[arr, 1 - p, :, block(k)]
        return copy(at, at, opp_s.at[k], opp_r.at[k], dp=sib)

    def rd_copy(g):
        return copy(ps.at[sib, g], qd.at[g], rd_s.at[g], rd_r.at[g], dp=sib)

    def rza_copy(g):
        return copy(zs.at[g, 0], zr.at[g, 0], rza_s.at[g], rza_r.at[g], tensor=right)

    def rzb_copy(g):
        return copy(zs.at[g, 1], zr.at[g, 1], rzb_s.at[g], rzb_r.at[g], tensor=left)

    def rx_copy(k, to=peer):
        return copy(xs.at[:, block(k)], tr.at[:, block(k)], rx_s.at[k], rx_r.at[k], expert=to)

    def rg_copy(k, to=peer):
        return copy(gd_out.at[block(k)], gd_in.at[block(k)], rg_s.at[k], rg_r.at[k], expert=to)

    def product(a, weights, rows):
        total = None
        for par in range(2):
            wide = jnp.concatenate([xd[a, par, m, rows] for m in range(4)], axis=1)
            term = jnp.dot(wide, weights[par], preferred_element_type=F32)
            total = term if total is None else total + term
        return total

    def compute_up(g):
        @pl.when(g == 0)
        def _():
            for made in weight_copies():
                made.wait()

        up_s[...] = product(0, wu, group_rows(g))

    def compute_down(g):
        rows = group_rows(g)
        for i in range(PER):
            k = g * PER + i

            @pl.when(k > 0)
            def _():
                gate_copy(k).wait_recv()

        dhid = product(1, wd, rows)
        up = up_s[...]
        gate = gate_in[rows].astype(F32)
        s = 1.0 / (1.0 + jnp.exp(-gate))
        act = gate * s
        hid[rows] = (act * up).astype(BF16)
        upd[rows] = (dhid * act).astype(BF16)
        delta = (dhid * up * (s * (1.0 + gate * (1.0 - s)))).astype(BF16)
        gd_out[rows] = delta

        @pl.when(g == 0)
        def _():
            gd_in[0:CAP] = delta[0:CAP]

        for i in range(PER):
            k = g * PER + i

            @pl.when(k > 0)
            def _():
                rg_copy(k, partner(me, k)).start()

    def compute_partial(g):
        value = upd[group_rows(g)]
        for m in range(4):
            for par in range(2):
                ps[m % 2, g, par, m // 2] = lax.dot_general(
                    value, wu[par, m * CH : (m + 1) * CH], NT, preferred_element_type=F32
                ).astype(BF16)
        rd_copy(g).start()

    def return_z(g):
        rd_copy(g).wait_recv()
        for mm in range(2):
            total = ps[c, g, 1 - p, mm].astype(F32) + qd[g, 1 - p, mm].astype(F32)
            zs[g, mm] = total.astype(BF16)
        rza_copy(g).start()
        rzb_copy(g).start()

    def return_xy(g):
        rza_copy(g).wait_recv()
        rzb_copy(g).wait_recv()
        rows = group_rows(g)
        for mm in range(2):
            total = ps[c, g, p, mm].astype(F32) + qd[g, p, mm].astype(F32) + zr[g, mm].astype(F32)
            value = total.astype(BF16)
            xs[mm, rows] = value

            @pl.when(g == 0)
            def _():
                tr[mm, 0:CAP] = value[0:CAP]

        for i in range(PER):
            k = g * PER + i

            @pl.when(k > 0)
            def _():
                rx_copy(k, partner(me, k)).start()

    def grad(a, par, m):
        right_side = (upd if a == 0 else hid)[...]
        q = 2 * m + par
        rows = slice(q * CH, (q + 1) * CH)
        grads[a, rows] = lax.dot_general(xd[a, par, m], right_side, TN, preferred_element_type=F32).astype(BF16)
        grad_copy(a, q).start()

    def grad_copy(a, q):
        rows = pl.ds(q * CH, CH)
        return pltpu.make_async_copy(grads.at[a, rows], (ug_hbm, dg_hbm)[a].at[0, rows], out_sem.at[a * 8 + q])

    jobs = [(a, par, m) for a in range(2) for m in range(4) for par in range(2)]
    LAG_Z, LAG_S, LAG_C = 2, 3, 3
    FIRST = PER - 1 + LAG_C

    @pl.loop(0, FIRST + PER * GROUPS)
    def _(step):
        @pl.when(step < NE)
        def _():
            @pl.when(step > 0)
            def _():
                for m in range(4):
                    xy_copy(step, m).wait_recv()

            za_copy(step, p).start()
            zb_copy(step, p).start()
            own_copy(step, c).start()

            @pl.when(step + WINDOW < NE)
            def _():
                send(step + WINDOW)

        @pl.when((step >= LAG_Z) & (step < NE + LAG_Z))
        def _():
            k = step - LAG_Z
            za_copy(k, 1 - p).wait_recv()
            zb_copy(k, 1 - p).wait_recv()
            opp_copy(k, c).start()

        @pl.when((step >= LAG_S) & (step < NE + LAG_S))
        def _():
            k = step - LAG_S
            own_copy(k, sib).wait_recv()
            opp_copy(k, sib).wait_recv()

        @pl.when(step >= FIRST)
        def _():
            turn = step - FIRST
            g = lax.div(turn, PER)
            phase = lax.rem(turn, PER)

            @pl.when(phase == 0)
            def _():
                compute_up(g)
                compute_down(g)

                @pl.when(g > 0)
                def _():
                    return_z(g - 1)

            @pl.when(phase == 1)
            def _():
                compute_partial(g)

                @pl.when(g > 0)
                def _():
                    return_xy(g - 1)

    last = GROUPS - 1
    for job in jobs[0:0]:
        grad(*job)
    return_z(last)
    for job in jobs[0:3]:
        grad(*job)
    return_xy(last)
    for job in jobs[3:12]:
        grad(*job)

    @pl.loop(1, NE)
    def _(k):
        rx_copy(k).wait_recv()

    def fin_dest(mm):
        return 2 * (c + 2 * mm) + p

    def fin_copy(mm, h):
        return copy(
            tk.at[mm, h], fr.at[mz], fin_s.at[mm * 2 + h], fin_r.at[mz], tensor=fin_dest(mm), dp=jnp.int32(h)
        )

    def fin_local(mm, h):
        return (fin_dest(mm) == z) & (c == h)

    for mm in range(2):
        total = lax.dot_general(s_tok[...], tr[mm], TN, preferred_element_type=F32).T
        for h in range(2):
            value = total[h * 192 : (h + 1) * 192].astype(BF16)
            tk[mm, h] = value

            @pl.when(fin_local(mm, h))
            def _():
                fr[mz] = value

            @pl.when(jnp.logical_not(fin_local(mm, h)))
            def _():
                fin_copy(mm, h).start()

    for job in jobs[12:16]:
        grad(*job)

    @pl.loop(1, NE)
    def _(k):
        rg_copy(k).wait_recv()

    gg_ref[...] = (
        lax.dot_general(s_route[...], gd_in[...], TN, preferred_element_type=F32).astype(BF16).reshape(TOK, 4, CH)
    )

    for j in range(4):
        token_copy(j, sib).wait_send()
        if j > 0:
            token_copy(j, c).wait_send()

    @pl.loop(0, NE)
    def _(k):
        za_copy(k, p).wait_send()
        zb_copy(k, p).wait_send()
        own_copy(k, c).wait_send()
        opp_copy(k, c).wait_send()

        @pl.when(k > 0)
        def _():
            gate_copy(k).wait_send()
            for m in range(4):
                xy_copy(k, m).wait_send()
            rx_copy(k).wait_send()
            rg_copy(k).wait_send()

    @pl.loop(0, GROUPS)
    def _(g):
        rd_copy(g).wait_send()
        rza_copy(g).wait_send()
        rzb_copy(g).wait_send()

    for a in range(2):
        for q in range(8):
            grad_copy(a, q).wait()

    for src in range(4):
        @pl.when(jnp.logical_not((mz == src) & (c == lax.rem(mz, 2))))
        def _():
            copy(
                fr.at[src], fr.at[src], fin_s.at[0], fin_r.at[src], tensor=right
            ).wait_recv()

    total = inp[1].astype(F32)
    for src in range(4):
        total = total + fr[src].astype(F32)
    ig_ref[...] = total.astype(BF16)

    for mm in range(2):
        for h in range(2):
            @pl.when(jnp.logical_not(fin_local(mm, h)))
            def _():
                fin_copy(mm, h).wait_send()


def finish(ig_in, gg_in, ug_in, dg_in, ig, gg, ug, dg, ig_v, gg_v, ug_v, dg_v, sem_in, sem_out):
    inward, outward = [], []
    for src, mid, dst, parts in (
        (ug_in, ug_v, ug, 4), (dg_in, dg_v, dg, 4), (gg_in, gg_v, gg, 1), (ig_in, ig_v, ig, 1)
    ):
        size = src.shape[1] // parts
        for part in range(parts):
            at = (0, pl.ds(part * size, size)) if parts > 1 else slice(None)
            n = len(inward)
            inward.append(pltpu.make_async_copy(src.at[at], mid.at[at], sem_in.at[n]))
            outward.append(pltpu.make_async_copy(mid.at[at], dst.at[at], sem_out.at[n]))
    for made in inward:
        made.start()
    for arrived, made in zip(inward, outward):
        arrived.wait()
        made.start()
    for made in outward:
        made.wait()


def local(moe_input, grad_out, expert_ids, route_weight, gate_pre, up_weight, down_weight):
    vmem = pl.BlockSpec(memory_space=pltpu.VMEM)
    anywhere = pl.BlockSpec(memory_space=pl.ANY)
    dma = pltpu.SemaphoreType.DMA

    def scratch(*shape, dtype=BF16):
        return pltpu.VMEM(shape, dtype)

    results = pl.pallas_call(
        kernel,
        out_shape=(
            jax.ShapeDtypeStruct((192, TOK), BF16),
            jax.ShapeDtypeStruct((TOK, 4, CH), BF16),
            jax.ShapeDtypeStruct(up_weight.shape, BF16),
            jax.ShapeDtypeStruct(down_weight.shape, BF16),
        ),
        in_specs=[anywhere] * 7,
        out_specs=(vmem, vmem, anywhere, anywhere),
        scratch_shapes=[
            scratch(2, 192, TOK),
            scratch(4, TOK, dtype=jnp.int32),
            scratch(4, TOK, dtype=F32),
            scratch(TOK, 4, CH),
            scratch(2, 4 * CH, CH),
            scratch(2, 4 * CH, CH),
            scratch(ROWS, TOK),
            scratch(ROWS, 4 * TOK),
            scratch(ROWS, TOK, dtype=F32),
            scratch(4, CH, TOK),
            scratch(4, TOK, CH),
            scratch(4, ROWS, CH),
            scratch(2, 2, 4, ROWS, CH),
            scratch(ROWS, CH),
            scratch(ROWS, CH),
            scratch(ROWS, CH),
            scratch(ROWS, CH),
            scratch(GROUP, CH, dtype=F32),
            scratch(ROWS, CH),
            scratch(ROWS, CH),
            scratch(2, GROUPS, 2, 2, GROUP, CH),
            scratch(GROUPS, 2, 2, GROUP, CH),
            scratch(GROUPS, 2, GROUP, CH),
            scratch(GROUPS, 2, GROUP, CH),
            scratch(2, ROWS, CH),
            scratch(2, ROWS, CH),
            scratch(2, 2, 192, TOK),
            scratch(4, 192, TOK),
            scratch(2, 8 * CH, CH),
            dma((5,)),
            dma((16,)),
            dma((8,)), dma((8,)),
            dma((NE,)), dma((NE,)),
            dma((4 * NE,)), dma((4 * NE,)),
            dma((NE,)), dma((NE,)),
            dma((NE,)), dma((NE,)),
            dma((NE,)), dma((NE,)),
            dma((NE,)), dma((NE,)),
            dma((GROUPS,)), dma((GROUPS,)),
            dma((GROUPS,)), dma((GROUPS,)),
            dma((GROUPS,)), dma((GROUPS,)),
            dma((NE,)), dma((NE,)),
            dma((NE,)), dma((NE,)),
            dma((4,)), dma((4,)),
            dma((16,)),
        ],
        compiler_params=pltpu.CompilerParams(
            collective_id=0, has_side_effects=True, vmem_limit_bytes=60 * 1024 * 1024
        ),
        name="routed_backward",
    )(moe_input.T, grad_out.T, expert_ids.T, route_weight.T, gate_pre, up_weight, down_weight)
    input_grad, gate_grad, up_grad, down_grad = pl.pallas_call(
        finish,
        out_shape=tuple(jax.ShapeDtypeStruct(r.shape, r.dtype) for r in results),
        in_specs=[anywhere] * 4,
        out_specs=(anywhere,) * 4,
        scratch_shapes=[scratch(*r.shape) for r in results] + [dma((10,)), dma((10,))],
        compiler_params=pltpu.CompilerParams(vmem_limit_bytes=60 * 1024 * 1024),
        name="results",
    )(*results)
    return input_grad.T, gate_grad, up_grad, down_grad


def solution(mesh):
    sharded = P("expert", ("tensor", "dp"))
    cube = P("expert", None, ("tensor", "dp"))
    rows = P("expert", None)
    return jax.shard_map(
        local,
        mesh=mesh,
        in_specs=(sharded, sharded, rows, rows, cube, cube, cube),
        out_specs=(sharded, cube, cube, cube),
        check_vma=False,
    )
```

```python
import functools

import jax
import jax.numpy as jnp
from jax import lax
from jax.experimental import pallas as pl
from jax.experimental.pallas import tpu as pltpu
from jax.sharding import PartitionSpec as P

MESH = pl.DeviceIdType.MESH
F32 = jnp.float32
BF16 = jnp.bfloat16
NE = 16
CAP = 64
TOK = 128
ROWS = NE * CAP
CH = 384
GROUP = 128
FILL = 256
WINDOW = 8
GROUPS = ROWS // GROUP
PER = GROUP // CAP
NT = (((1,), (1,)), ((), ()))
TN = (((0,), (0,)), ((), ()))


def partner(me, k):
    k0, k1, k2, k3 = (lax.rem(lax.div(k, bit), 2) for bit in (1, 2, 4, 8))
    flips = (k0 + k1 + k2, k1 + k3, k0 + k1, k1)
    total = 0
    for i, flip in enumerate(flips):
        total = total + 2**i * lax.rem(lax.div(me, 2**i) + flip, 2)
    return total


def block(k):
    return pl.ds(pl.multiple_of(k * CAP, CAP), CAP)


def group_rows(g):
    return pl.ds(pl.multiple_of(g * GROUP, GROUP), GROUP)


def kernel(
    x_hbm, g_hbm, ids_hbm, w_hbm, gate_hbm, wu_hbm, wd_hbm,
    ig_ref, gg_ref, ug_hbm, dg_hbm,
    inp, ids_ref, w_ref, gate_ref,
    wu, wd, s_tok, s_route, w_slot, t4, t4_t, slots, xd,
    gate_out, gate_in, gd_out, gd_in, up_s, hid, upd, ps, qd, zs, zr, xs, tr, tk, fr, grads,
    in_sem, w_sem, a1_s, a1_r, gate_s, gate_r, xy_s, xy_r, za_s, za_r, zb_s, zb_r,
    own_s, own_r, opp_s, opp_r, rd_s, rd_r, rza_s, rza_r, rzb_s, rzb_r, rx_s, rx_r,
    rg_s, rg_r, fin_s, fin_r, out_sem,
):
    me = lax.axis_index("expert")
    z = lax.axis_index("tensor")
    c = lax.axis_index("dp")
    p = lax.rem(z, 2)
    mz = lax.div(z, 2)
    sib = 1 - c
    right = lax.rem(z + 1, 8)
    left = lax.rem(z + 7, 8)

    def copy(src, dst, send, recv, **ids):
        return pltpu.make_async_remote_copy(
            src_ref=src, dst_ref=dst, send_sem=send, recv_sem=recv, device_id=ids, device_id_type=MESH
        )

    loads = [
        pltpu.make_async_copy(src, dst, in_sem.at[i])
        for i, (src, dst) in enumerate(
            ((ids_hbm, ids_ref), (w_hbm, w_ref), (x_hbm, inp.at[0]), (g_hbm, inp.at[1]), (gate_hbm, gate_ref))
        )
    ]
    for load in loads:
        load.start()

    bar = pltpu.get_barrier_semaphore()

    def greet(**ids):
        pl.semaphore_signal(bar, inc=1, device_id=ids, device_id_type=MESH)

    greet(dp=sib)
    for j in range(1, 4):
        greet(tensor=lax.rem(z + 2 * j, 8))
        greet(tensor=lax.rem(z + 2 * j, 8), dp=sib)
    greet(tensor=right)
    greet(tensor=left)

    @pl.loop(1, NE)
    def _(k):
        greet(expert=partner(me, k))

    def weight_copies():
        made = []
        for i, (src, dst) in enumerate(((wu_hbm, wu), (wd_hbm, wd))):
            for q in range(8):
                made.append(
                    pltpu.make_async_copy(
                        src.at[0, pl.ds(q * CH, CH)],
                        dst.at[q % 2, pl.ds((q // 2) * CH, CH)],
                        w_sem.at[i * 8 + q],
                    )
                )
        return made

    for made in weight_copies():
        made.start()

    loads[0].wait()
    loads[1].wait()
    lane = lax.broadcasted_iota(jnp.int32, (TOK, TOK), 1)
    sub = lax.broadcasted_iota(jnp.int32, (TOK, TOK), 0)
    earlier = (sub < lane).astype(BF16)
    lane4 = lax.broadcasted_iota(jnp.int32, (TOK, 4 * TOK), 1)
    sub4 = 4 * lax.broadcasted_iota(jnp.int32, (TOK, 4 * TOK), 0)
    spread = ((lane4 >= sub4) & (lane4 < sub4 + 4)).astype(BF16)
    ids = ids_ref[...].astype(F32)
    wts = w_ref[...]
    experts = [partner(me, jnp.int32(k)).astype(F32) for k in range(NE)]
    hits = [[(ids[j : j + 1] == experts[k]).astype(F32) for j in range(4)] for k in range(NE)]
    named = jnp.concatenate([h[0] + h[1] + h[2] + h[3] for h in hits], axis=0)
    rank = jnp.dot(named.astype(BF16), earlier, preferred_element_type=F32)
    rank4 = jnp.dot(rank.astype(BF16), spread, preferred_element_type=F32)
    ids_wide = jnp.dot(
        jnp.concatenate([ids, ids], axis=0).astype(BF16), spread, preferred_element_type=F32
    )
    route = lax.rem(lax.broadcasted_iota(jnp.int32, (1, 4 * TOK), 1), 4)
    ids4 = jnp.zeros((1, 4 * TOK), F32)
    for j in range(4):
        ids4 = jnp.where(route == j, ids_wide[j : j + 1], ids4)
    place = lax.broadcasted_iota(jnp.int32, (CAP, TOK), 0).astype(F32)
    place4 = lax.broadcasted_iota(jnp.int32, (CAP, 4 * TOK), 0).astype(F32)
    for k in range(NE):
        here = jnp.where((rank[k : k + 1] == place) & (named[k : k + 1] > 0.5), 1.0, 0.0)
        rows = slice(k * CAP, (k + 1) * CAP)
        s_tok[rows] = here.astype(BF16)
        weight = jnp.zeros((1, TOK), F32)
        for j in range(4):
            weight = weight + hits[k][j] * wts[j : j + 1]
        col = jnp.sum(here * weight, axis=1, keepdims=True)
        w_slot[rows] = jnp.where(c == 0, jnp.ones((CAP, TOK), F32), jnp.broadcast_to(col, (CAP, TOK)))
        here4 = jnp.where((rank4[k : k + 1] == place4) & (ids4 == experts[k]), 1.0, 0.0)
        s_route[rows] = here4.astype(BF16)

    loads[2].wait()
    loads[3].wait()

    def half(i):
        return pl.ds(pl.multiple_of(192 * i, 192), 192)

    t4[mz, half(c)] = inp[c]
    pl.semaphore_wait(bar, 24)

    def token_copy(j, h):
        return copy(
            inp.at[h], t4.at[mz, half(c)], a1_s.at[2 * j + h], a1_r.at[2 * j + c], tensor=lax.rem(z + 2 * j, 8), dp=h
        )

    def token_arrival(j, h):
        src = lax.rem(mz + 4 - j, 4)
        return copy(
            inp.at[h], t4.at[src, half(h)], a1_s.at[2 * j + h], a1_r.at[2 * j + h], tensor=right, dp=sib
        )

    token_copy(0, sib).start()
    for j in (2, 1, 3):
        token_copy(j, c).start()
        token_copy(j, sib).start()
    token_arrival(0, sib).wait_recv()

    peer = lax.rem(me + 1, NE)

    def xy_copy(k, m, to=peer):
        at = 4 * k + m
        return copy(slots.at[m, block(k)], xd.at[c, p, m, block(k)], xy_s.at[at], xy_r.at[at], expert=to)

    def fill(g, m):
        rows = pl.ds(pl.multiple_of(g * FILL, FILL), FILL)
        value = jnp.dot(s_tok[rows], t4_t[m], preferred_element_type=F32)
        scale = w_slot[rows]
        value = (value * jnp.concatenate([scale] * (CH // TOK), axis=1)).astype(BF16)
        slots[m, rows] = value

        @pl.when(g == 0)
        def _():
            xd[c, p, m, 0:CAP] = value[0:CAP]

    def gate_copy(k, to=peer):
        return copy(gate_out.at[block(k)], gate_in.at[block(k)], gate_s.at[k], gate_r.at[k], expert=to)

    t4_t[mz] = t4[mz].T

    @pl.loop(0, ROWS // FILL)
    def _(g):
        fill(g, mz)
        for i in range(FILL // CAP):
            k = g * (FILL // CAP) + i

            @pl.when(k > 0)
            def _():
                xy_copy(k, mz, partner(me, k)).start()

    loads[4].wait()
    gate_rows = gate_ref[...].reshape(4 * TOK, CH)
    for g in range(4):
        value = jnp.dot(s_route[g * 256 : (g + 1) * 256], gate_rows, preferred_element_type=F32).astype(BF16)
        gate_out[g * 256 : (g + 1) * 256] = value
        if g == 0:
            gate_in[0:CAP] = value[0:CAP]
        if g == 1:
            for k in range(1, 5):
                gate_copy(jnp.int32(k), partner(me, jnp.int32(k))).start()

    for j in (1, 3, 2):
        for h in range(2):
            token_arrival(j, h).wait_recv()
    for j in (1, 3, 2):
        src = lax.rem(mz + 4 - j, 4)
        t4_t[src] = t4[src].T

    def others():
        return [lax.rem(mz + j, 4) for j in (1, 2, 3)]

    def send(k):
        to = partner(me, k)
        for m in others():
            xy_copy(k, m, to).start()

        @pl.when(k > 4)
        def _():
            gate_copy(k, to).start()

    @pl.loop(0, ROWS // FILL)
    def _(g):
        for m in others():
            fill(g, m)
        for i in range(FILL // CAP):
            k = g * (FILL // CAP) + i

            @pl.when((k > 0) & (k < WINDOW))
            def _():
                send(k)

    def za_copy(k, par):
        at = xd.at[c, par, pl.ds(0, 2), block(k)]
        return copy(at, at, za_s.at[k], za_r.at[k], tensor=right)

    def zb_copy(k, par):
        at = xd.at[c, par, pl.ds(2, 2), block(k)]
        return copy(at, at, zb_s.at[k], zb_r.at[k], tensor=left)

    def own_copy(k, arr):
        at = xd.at[arr, p, :, block(k)]
        return copy(at, at, own_s.at[k], own_r.at[k], dp=sib)

    def opp_copy(k, arr):
        at = xd.at[arr, 1 - p, :, block(k)]
        return copy(at, at, opp_s.at[k], opp_r.at[k], dp=sib)

    def rd_copy(g):
        return copy(ps.at[sib, g], qd.at[g], rd_s.at[g], rd_r.at[g], dp=sib)

    def rza_copy(g):
        return copy(zs.at[g, 0], zr.at[g, 0], rza_s.at[g], rza_r.at[g], tensor=right)

    def rzb_copy(g):
        return copy(zs.at[g, 1], zr.at[g, 1], rzb_s.at[g], rzb_r.at[g], tensor=left)

    def rx_copy(k, to=peer):
        return copy(xs.at[:, block(k)], tr.at[:, block(k)], rx_s.at[k], rx_r.at[k], expert=to)

    def rg_copy(k, to=peer):
        return copy(gd_out.at[block(k)], gd_in.at[block(k)], rg_s.at[k], rg_r.at[k], expert=to)

    def product(a, weights, rows):
        total = None
        for par in range(2):
            wide = jnp.concatenate([xd[a, par, m, rows] for m in range(4)], axis=1)
            term = jnp.dot(wide, weights[par], preferred_element_type=F32)
            total = term if total is None else total + term
        return total

    def compute_up(g):
        @pl.when(g == 0)
        def _():
            for made in weight_copies():
                made.wait()

        up_s[...] = product(0, wu, group_rows(g))

    def compute_down(g):
        rows = group_rows(g)
        for i in range(PER):
            k = g * PER + i

            @pl.when(k > 0)
            def _():
                gate_copy(k).wait_recv()

        dhid = product(1, wd, rows)
        up = up_s[...]
        gate = gate_in[rows].astype(F32)
        s = 1.0 / (1.0 + jnp.exp(-gate))
        act = gate * s
        hid[rows] = (act * up).astype(BF16)
        upd[rows] = (dhid * act).astype(BF16)
        delta = (dhid * up * (s * (1.0 + gate * (1.0 - s)))).astype(BF16)
        gd_out[rows] = delta

        @pl.when(g == 0)
        def _():
            gd_in[0:CAP] = delta[0:CAP]

        for i in range(PER):
            k = g * PER + i

            @pl.when(k > 0)
            def _():
                rg_copy(k, partner(me, k)).start()

    def compute_partial(g):
        value = upd[group_rows(g)]
        for m in range(4):
            for par in range(2):
                ps[m % 2, g, par, m // 2] = lax.dot_general(
                    value, wu[par, m * CH : (m + 1) * CH], NT, preferred_element_type=F32
                ).astype(BF16)
        rd_copy(g).start()

    def return_z(g):
        rd_copy(g).wait_recv()
        for mm in range(2):
            total = ps[c, g, 1 - p, mm].astype(F32) + qd[g, 1 - p, mm].astype(F32)
            zs[g, mm] = total.astype(BF16)
        rza_copy(g).start()
        rzb_copy(g).start()

    def return_xy(g):
        rza_copy(g).wait_recv()
        rzb_copy(g).wait_recv()
        rows = group_rows(g)
        for mm in range(2):
            total = ps[c, g, p, mm].astype(F32) + qd[g, p, mm].astype(F32) + zr[g, mm].astype(F32)
            value = total.astype(BF16)
            xs[mm, rows] = value

            @pl.when(g == 0)
            def _():
                tr[mm, 0:CAP] = value[0:CAP]

        for i in range(PER):
            k = g * PER + i

            @pl.when(k > 0)
            def _():
                rx_copy(k, partner(me, k)).start()

    def grad(a, par, m):
        right_side = (upd if a == 0 else hid)[...]
        q = 2 * m + par
        rows = slice(q * CH, (q + 1) * CH)
        grads[a, rows] = lax.dot_general(xd[a, par, m], right_side, TN, preferred_element_type=F32).astype(BF16)
        grad_copy(a, q).start()

    def grad_copy(a, q):
        rows = pl.ds(q * CH, CH)
        return pltpu.make_async_copy(grads.at[a, rows], (ug_hbm, dg_hbm)[a].at[0, rows], out_sem.at[a * 8 + q])

    jobs = [(a, par, m) for a in range(2) for m in range(4) for par in range(2)]
    LAG_Z, LAG_S, LAG_C = 2, 3, 3
    FIRST = PER - 1 + LAG_C

    @pl.loop(0, FIRST + PER * GROUPS)
    def _(step):
        @pl.when(step < NE)
        def _():
            @pl.when(step > 0)
            def _():
                for m in range(4):
                    xy_copy(step, m).wait_recv()

            za_copy(step, p).start()
            zb_copy(step, p).start()
            own_copy(step, c).start()

            @pl.when(step + WINDOW < NE)
            def _():
                send(step + WINDOW)

        @pl.when((step >= LAG_Z) & (step < NE + LAG_Z))
        def _():
            k = step - LAG_Z
            za_copy(k, 1 - p).wait_recv()
            zb_copy(k, 1 - p).wait_recv()
            opp_copy(k, c).start()

        @pl.when((step >= LAG_S) & (step < NE + LAG_S))
        def _():
            k = step - LAG_S
            own_copy(k, sib).wait_recv()
            opp_copy(k, sib).wait_recv()

        @pl.when(step >= FIRST)
        def _():
            turn = step - FIRST
            g = lax.div(turn, PER)
            phase = lax.rem(turn, PER)

            @pl.when(phase == 0)
            def _():
                compute_up(g)

                @pl.when(g > 0)
                def _():
                    return_z(g - 1)

                compute_down(g)

            @pl.when(phase == 1)
            def _():
                compute_partial(g)

                @pl.when(g > 0)
                def _():
                    return_xy(g - 1)

    last = GROUPS - 1
    for job in jobs[0:0]:
        grad(*job)
    return_z(last)
    for job in jobs[0:3]:
        grad(*job)
    return_xy(last)
    for job in jobs[3:12]:
        grad(*job)

    @pl.loop(1, NE)
    def _(k):
        rx_copy(k).wait_recv()

    def fin_dest(mm):
        return 2 * (c + 2 * mm) + p

    def fin_copy(mm, h):
        return copy(
            tk.at[mm, h], fr.at[mz], fin_s.at[mm * 2 + h], fin_r.at[mz], tensor=fin_dest(mm), dp=jnp.int32(h)
        )

    def fin_local(mm, h):
        return (fin_dest(mm) == z) & (c == h)

    for mm in range(2):
        total = lax.dot_general(s_tok[...], tr[mm], TN, preferred_element_type=F32).T
        for h in range(2):
            value = total[h * 192 : (h + 1) * 192].astype(BF16)
            tk[mm, h] = value

            @pl.when(fin_local(mm, h))
            def _():
                fr[mz] = value

            @pl.when(jnp.logical_not(fin_local(mm, h)))
            def _():
                fin_copy(mm, h).start()

    for job in jobs[12:16]:
        grad(*job)

    @pl.loop(1, NE)
    def _(k):
        rg_copy(k).wait_recv()

    gg_ref[...] = (
        lax.dot_general(s_route[...], gd_in[...], TN, preferred_element_type=F32).astype(BF16).reshape(TOK, 4, CH)
    )

    for j in range(4):
        token_copy(j, sib).wait_send()
        if j > 0:
            token_copy(j, c).wait_send()

    @pl.loop(0, NE)
    def _(k):
        za_copy(k, p).wait_send()
        zb_copy(k, p).wait_send()
        own_copy(k, c).wait_send()
        opp_copy(k, c).wait_send()

        @pl.when(k > 0)
        def _():
            gate_copy(k).wait_send()
            for m in range(4):
                xy_copy(k, m).wait_send()
            rx_copy(k).wait_send()
            rg_copy(k).wait_send()

    @pl.loop(0, GROUPS)
    def _(g):
        rd_copy(g).wait_send()
        rza_copy(g).wait_send()
        rzb_copy(g).wait_send()

    for a in range(2):
        for q in range(8):
            grad_copy(a, q).wait()

    for src in range(4):
        @pl.when(jnp.logical_not((mz == src) & (c == lax.rem(mz, 2))))
        def _():
            copy(
                fr.at[src], fr.at[src], fin_s.at[0], fin_r.at[src], tensor=right
            ).wait_recv()

    total = inp[1].astype(F32)
    for src in range(4):
        total = total + fr[src].astype(F32)
    ig_ref[...] = total.astype(BF16)

    for mm in range(2):
        for h in range(2):
            @pl.when(jnp.logical_not(fin_local(mm, h)))
            def _():
                fin_copy(mm, h).wait_send()


def finish(ig_in, gg_in, ug_in, dg_in, ig, gg, ug, dg, ig_v, gg_v, ug_v, dg_v, sem_in, sem_out):
    inward, outward = [], []
    for src, mid, dst, parts in (
        (ug_in, ug_v, ug, 4), (dg_in, dg_v, dg, 4), (gg_in, gg_v, gg, 1), (ig_in, ig_v, ig, 1)
    ):
        size = src.shape[1] // parts
        for part in range(parts):
            at = (0, pl.ds(part * size, size)) if parts > 1 else slice(None)
            n = len(inward)
            inward.append(pltpu.make_async_copy(src.at[at], mid.at[at], sem_in.at[n]))
            outward.append(pltpu.make_async_copy(mid.at[at], dst.at[at], sem_out.at[n]))
    for made in inward:
        made.start()
    for arrived, made in zip(inward, outward):
        arrived.wait()
        made.start()
    for made in outward:
        made.wait()


def local(moe_input, grad_out, expert_ids, route_weight, gate_pre, up_weight, down_weight):
    vmem = pl.BlockSpec(memory_space=pltpu.VMEM)
    anywhere = pl.BlockSpec(memory_space=pl.ANY)
    dma = pltpu.SemaphoreType.DMA

    def scratch(*shape, dtype=BF16):
        return pltpu.VMEM(shape, dtype)

    results = pl.pallas_call(
        kernel,
        out_shape=(
            jax.ShapeDtypeStruct((192, TOK), BF16),
            jax.ShapeDtypeStruct((TOK, 4, CH), BF16),
            jax.ShapeDtypeStruct(up_weight.shape, BF16),
            jax.ShapeDtypeStruct(down_weight.shape, BF16),
        ),
        in_specs=[anywhere] * 7,
        out_specs=(vmem, vmem, anywhere, anywhere),
        scratch_shapes=[
            scratch(2, 192, TOK),
            scratch(4, TOK, dtype=jnp.int32),
            scratch(4, TOK, dtype=F32),
            scratch(TOK, 4, CH),
            scratch(2, 4 * CH, CH),
            scratch(2, 4 * CH, CH),
            scratch(ROWS, TOK),
            scratch(ROWS, 4 * TOK),
            scratch(ROWS, TOK, dtype=F32),
            scratch(4, CH, TOK),
            scratch(4, TOK, CH),
            scratch(4, ROWS, CH),
            scratch(2, 2, 4, ROWS, CH),
            scratch(ROWS, CH),
            scratch(ROWS, CH),
            scratch(ROWS, CH),
            scratch(ROWS, CH),
            scratch(GROUP, CH, dtype=F32),
            scratch(ROWS, CH),
            scratch(ROWS, CH),
            scratch(2, GROUPS, 2, 2, GROUP, CH),
            scratch(GROUPS, 2, 2, GROUP, CH),
            scratch(GROUPS, 2, GROUP, CH),
            scratch(GROUPS, 2, GROUP, CH),
            scratch(2, ROWS, CH),
            scratch(2, ROWS, CH),
            scratch(2, 2, 192, TOK),
            scratch(4, 192, TOK),
            scratch(2, 8 * CH, CH),
            dma((5,)),
            dma((16,)),
            dma((8,)), dma((8,)),
            dma((NE,)), dma((NE,)),
            dma((4 * NE,)), dma((4 * NE,)),
            dma((NE,)), dma((NE,)),
            dma((NE,)), dma((NE,)),
            dma((NE,)), dma((NE,)),
            dma((NE,)), dma((NE,)),
            dma((GROUPS,)), dma((GROUPS,)),
            dma((GROUPS,)), dma((GROUPS,)),
            dma((GROUPS,)), dma((GROUPS,)),
            dma((NE,)), dma((NE,)),
            dma((NE,)), dma((NE,)),
            dma((4,)), dma((4,)),
            dma((16,)),
        ],
        compiler_params=pltpu.CompilerParams(
            collective_id=0, has_side_effects=True, vmem_limit_bytes=60 * 1024 * 1024
        ),
        name="routed_backward",
    )(moe_input.T, grad_out.T, expert_ids.T, route_weight.T, gate_pre, up_weight, down_weight)
    input_grad, gate_grad, up_grad, down_grad = pl.pallas_call(
        finish,
        out_shape=tuple(jax.ShapeDtypeStruct(r.shape, r.dtype) for r in results),
        in_specs=[anywhere] * 4,
        out_specs=(anywhere,) * 4,
        scratch_shapes=[scratch(*r.shape) for r in results] + [dma((10,)), dma((10,))],
        compiler_params=pltpu.CompilerParams(vmem_limit_bytes=60 * 1024 * 1024),
        name="results",
    )(*results)
    return input_grad.T, gate_grad, up_grad, down_grad


def solution(mesh):
    sharded = P("expert", ("tensor", "dp"))
    cube = P("expert", None, ("tensor", "dp"))
    rows = P("expert", None)
    return jax.shard_map(
        local,
        mesh=mesh,
        in_specs=(sharded, sharded, rows, rows, cube, cube, cube),
        out_specs=(sharded, cube, cube, cube),
        check_vma=False,
    )
```
